512 devices in a mesh: ctx: 64 (over z, y), head: 8 (over x, core).
Axes of the slice: x: 4, y: 8, z: 8, core: 2. Of those that a mesh axis runs over, the one named last changes fastest.
Arguments:
- queries: bfloat16 [16384, 4096], P('ctx', 'head'), may hold values from -24 to 24
- keys: bfloat16 [16384, 4096], P('ctx', 'head'), may hold values from -6 to 6
- values: bfloat16 [16384, 4096], P('ctx', 'head'), may hold values from -72 to 72
- out_grad: bfloat16 [16384, 4096], P('ctx', 'head'), may hold values from -6 to 6
- gain: float32 [4096], P('head'), may hold values from 0.1 to 1.9
- segment_ids: int32 [16384], P('ctx'), may hold values from 0 to 7, never falling along the last dimension, each value on 1 to 8192 neighbouring positions
Outputs:
- grad_queries: bfloat16 [16384, 4096], P('ctx', 'head')
- grad_keys: bfloat16 [16384, 4096], P('ctx', 'head')
- grad_values: bfloat16 [16384, 4096], P('ctx', 'head')
The draws below stay inside these ranges and needn't reach their ends.
Inputs may be any that keep to these rules, and one draw needn't show every extreme that they name: `segment_ids`: ids never fall along the sequence; every document has 1 to 8192 tokens, one exactly that many.
All inputs are finite; a program needn't handle non-finite values.
Results may differ from the reference program's by a relative error of at most 0.0013.
Values sent between devices are 32-bit elements; how exact they have to be, the bound alone decides.
A program may use at most 128 MiB of HBM per device.

```python
import math
import jax
import jax.numpy as jnp
import numpy as np
from jax import lax

HD = 128
TOK_DEV = 256
DOCS = 8
HEADS = 32
TOKENS = 16384


def draw_queries(key, part):
    key = jax.random.fold_in(key, 5)
    key_rows, key_base = jax.random.split(key)
    features = HEADS * HD
    row_scale = 0.4 * jnp.exp(jax.random.uniform(key_rows, (TOKENS, 1), jnp.float32, 0.0, math.log(10.0)))
    base = jnp.clip(jax.random.normal(key_base, (TOKENS, features), jnp.float32), -6.0, 6.0)
    return (base * row_scale).astype(jnp.bfloat16)


def draw_values(key, part):
    key = jax.random.fold_in(key, 11)
    key_cols, key_base = jax.random.split(key, 2)
    features = HEADS * HD
    head_number = (jnp.arange(features) // HD).astype(jnp.float32)
    climb = 3.0 ** (head_number / max(HEADS - 1, 1))
    col_scale = jnp.exp(jax.random.uniform(key_cols, (features,), jnp.float32, 0.0, math.log(4.0)))
    base = jnp.clip(jax.random.normal(key_base, (TOKENS, features), jnp.float32), -6.0, 6.0)
    return (base * (climb * col_scale)[None, :]).astype(jnp.bfloat16)


def shard_levels(stream_key, shape, pieces, low, largest):
    loudness, own = 1.0, jax.random.fold_in(stream_key, 6)
    for dim, blocks in pieces:
        heights = jnp.exp(jax.random.uniform(jax.random.fold_in(own, dim), (blocks,), jnp.float32, low / len(pieces), largest / len(pieces)))
        loudness = loudness * jnp.repeat(heights, shape[dim] // blocks).reshape([-1 if axis == dim else 1 for axis in range(len(shape))])
    return loudness


def profile(amount, total, most, slope):
    portions = [(1 << 20) // math.isqrt(standing ** slope) + 1 for standing in range(2, amount + 1)]
    spare, holding = total - most - (amount - 1), [1] * (amount - 1)
    while spare > 0:
        movable = [i for i in range(amount - 1) if holding[i] < most]
        pool, remaining = sum([portions[i] for i in movable]), spare
        for i in movable:
            more = min(most - holding[i], max(1, remaining * portions[i] // pool), spare)
            holding[i] = holding[i] + more
            spare = spare - more
    return np.array([most] + holding)


def uneven_parts(key, count, total, reach, lean):
    if count == 2:
        one = jax.random.randint(key, (), max(1, total - reach), min(reach, total - 1) + 1)
        return jnp.stack([one, total - one])
    sizes = jnp.asarray(profile(count, total, reach, lean), jnp.int32)
    couples = (count - 1) // 2
    giver, sink = sizes[1:1 + 2 * couples:2], sizes[2:2 + 2 * couples:2]
    margin = jnp.minimum(giver - 1, reach - sink)
    shifted = jax.random.randint(jax.random.fold_in(key, 1), (couples,), 0, 1 << 20) % (margin + 1)
    sizes = sizes.at[1:1 + 2 * couples:2].set(giver - shifted).at[2:2 + 2 * couples:2].set(sink + shifted)
    return sizes[jax.random.permutation(jax.random.fold_in(key, 2), count)]


def centred(rng, shape, width, most, pieces=(), kind=jnp.bfloat16):
    level = shard_levels(rng, shape, pieces, -0.22, 0.18) if pieces else 1.0
    values = jax.random.normal(rng, shape, jnp.float32) * width * level
    return jnp.minimum(jnp.maximum(values, -most), most).astype(kind)


def setup_inputs(seed: int = 0) -> dict:
    arg_keys = jax.random.split(jax.random.key(seed), 7)
    return {
        "queries": draw_queries(jax.random.fold_in(arg_keys[6], 71), 0),
        "keys": centred(arg_keys[1], (TOKENS, HEADS * HD), 1.0, 6.0, ((0, 64), (1, 8))),
        "values": draw_values(jax.random.fold_in(arg_keys[6], 71), 0),
        "out_grad": centred(arg_keys[3], (TOKENS, HEADS * HD), 1.0, 6.0, ((0, 64), (1, 8))),
        "gain": jnp.clip(1.0 + 0.18 * jax.random.normal(arg_keys[4], (HEADS * HD,), jnp.float32), 0.1, 1.9),
        "segment_ids": jnp.searchsorted(jnp.cumsum(uneven_parts(arg_keys[5], DOCS, TOKENS, TOKENS // 2, 0)), jnp.arange(TOKENS), side="right").astype(jnp.int32),
    }


EPSILON = 1e-06

def join_states(earlier, latter):
    tag_early, state_early = earlier
    tag_late, state_late = latter
    is_empty = tag_late < 0
    same_doc = (tag_early == tag_late).astype(state_late.dtype)
    return (jnp.where(is_empty, tag_early, tag_late), jnp.where(is_empty, state_early, state_late + same_doc * state_early))

def visibility(doc_ids):
    position = jnp.arange(doc_ids.shape[0])
    return ((doc_ids[:, None] == doc_ids[None, :]) & (position[None, :] <= position[:, None])).astype(jnp.float32)

def reference(queries, keys, values, out_grad, gain, segment_ids):
    highest = lax.Precision.HIGHEST
    block = TOK_DEV // 4
    blocks = TOKENS // block
    features = HEADS * HD

    def to_blocks(array):
        return array.reshape(blocks, block, HEADS, HD)
    q_blocks = to_blocks(queries)
    k_blocks = to_blocks(keys)
    v_blocks = to_blocks(values)
    id_blocks = segment_ids.astype(jnp.float32).reshape(blocks, block)
    no_tag = jnp.float32(-1.0)
    zero_state = jnp.zeros((HEADS, HD, HD), jnp.float32)

    def forward_step(carry, inputs):
        q_b, k_b, v_b, ids_b = inputs
        tag_in, state_in = carry
        visible = visibility(ids_b)
        scores = jnp.einsum('thd,shd->hts', q_b, k_b, preferred_element_type=jnp.float32) * visible[None]
        q_wide = q_b.astype(jnp.float32)
        k_wide = k_b.astype(jnp.float32)
        v_wide = v_b.astype(jnp.float32)
        in_mask = (ids_b == tag_in).astype(jnp.float32)[:, None, None]
        attended = jnp.einsum('hts,she->the', scores, v_wide, precision=highest) + in_mask * jnp.einsum('thd,hde->the', q_wide, state_in, precision=highest)
        last_mask = (ids_b == ids_b[-1]).astype(jnp.float32)[:, None, None]
        tail_state = jnp.einsum('thd,the->hde', k_wide * last_mask, v_wide, precision=highest)
        joined = join_states(carry, (ids_b[-1], tail_state))
        return (joined, (attended, state_in, tag_in))
    final_state, (attended, states_in, tags_in) = lax.scan(forward_step, (no_tag, zero_state), (q_blocks, k_blocks, v_blocks, id_blocks))
    flat = attended.reshape(TOKENS, features)
    weighted = gain[None, :] * out_grad.astype(jnp.float32)
    inv_rms = lax.rsqrt(lax.optimization_barrier(jnp.mean(flat * flat, axis=1)) + EPSILON)
    cross = lax.optimization_barrier(jnp.mean(flat * weighted, axis=1))
    grad_flat = inv_rms[:, None] * (weighted - flat * (inv_rms * inv_rms * cross)[:, None])
    grad_blocks = grad_flat.reshape(blocks, block, HEADS, HD)

    def backward_step(carry, inputs):
        q_b, k_b, v_b, ids_b, grad_att, state_in, tag_in = inputs
        tag_back, grad_in = carry
        visible = visibility(ids_b)
        scores = jnp.einsum('thd,shd->hts', q_b, k_b, preferred_element_type=jnp.float32) * visible[None]
        q_wide = q_b.astype(jnp.float32)
        k_wide = k_b.astype(jnp.float32)
        v_wide = v_b.astype(jnp.float32)
        in_mask = (ids_b == tag_in).astype(jnp.float32)[:, None, None]
        out_mask = (ids_b == tag_back).astype(jnp.float32)[:, None, None]
        back_scores = jnp.einsum('the,she->hts', grad_att, v_wide, precision=highest) * visible[None]
        grad_q = jnp.einsum('hts,shd->thd', back_scores, k_wide, precision=highest) + in_mask * jnp.einsum('the,hde->thd', grad_att, state_in, precision=highest)
        grad_k = jnp.einsum('hts,thd->shd', back_scores, q_wide, precision=highest) + out_mask * jnp.einsum('she,hde->shd', v_wide, grad_in, precision=highest)
        grad_v = jnp.einsum('hts,the->she', scores, grad_att, precision=highest) + out_mask * jnp.einsum('shd,hde->she', k_wide, grad_in, precision=highest)
        first_mask = (ids_b == ids_b[0]).astype(jnp.float32)[:, None, None]
        head_sum = jnp.einsum('thd,the->hde', q_wide * first_mask, grad_att, precision=highest)
        joined = join_states(carry, (ids_b[0], head_sum))
        return (joined, (grad_q.astype(jnp.bfloat16), grad_k.astype(jnp.bfloat16), grad_v.astype(jnp.bfloat16)))
    final_back, (grad_q, grad_k, grad_v) = lax.scan(backward_step, (no_tag, zero_state), (q_blocks, k_blocks, v_blocks, id_blocks, grad_blocks, states_in, tags_in), reverse=True)
    return (grad_q.reshape(TOKENS, features), grad_k.reshape(TOKENS, features), grad_v.reshape(TOKENS, features))
```

```python
import functools

import jax
import jax.numpy as jnp
from jax import lax
from jax.experimental import pallas as pl
from jax.experimental.pallas import tpu as pltpu
from jax.sharding import PartitionSpec as P

HD = 128
EPSILON = 1e-06
RING = 8
MESH = pl.DeviceIdType.MESH
F32 = jnp.float32
BF16 = jnp.bfloat16


def dot(a, b, ca, cb):
    return lax.dot_general(a, b, (((ca,), (cb,)), ((), ())), preferred_element_type=F32)


def split(x):
    hi = x.astype(BF16)
    return hi, (x - hi.astype(F32)).astype(BF16)


def kernel(
    nctx, nhead, features,
    q_hbm, k_hbm, v_hbm, g_hbm, gain_ref, ids_ref,
    gq_hbm, gk_hbm, gv_hbm,
    q_ref, k_ref, v_ref, g_ref, oq_ref, ok_ref, ov_ref,
    snd, rcv, ps_snd, ps_rcv,
    sc_hi, sc_lo, att, wgt, gr_hi, gr_lo, st_hi, st_lo, lk, lv,
    in_sem, out_sem, send_sem, recv_sem, ps_sem,
):
    rows, width = q_ref.shape
    heads = width // HD
    piece = snd.shape[2] - 8
    nz = nctx // RING
    me = lax.axis_index("ctx")
    z, y = me // RING, me % RING
    h = lax.axis_index("head")

    offsets = [(dz, dy) for dz in range(nz) for dy in range(RING) if dz or dy]
    offsets.sort(key=lambda o: -(min(o[0], nz - o[0]) + min(o[1], RING - o[1])))
    peers = [lax.rem(z + dz, nz) * RING + lax.rem(y + dy, RING) for dz, dy in offsets]

    barrier = pltpu.get_barrier_semaphore()
    for p in peers:
        pl.semaphore_signal(barrier, inc=1, device_id={"ctx": p}, device_id_type=MESH)
    for d in range(1, nhead):
        pl.semaphore_signal(barrier, inc=1, device_id={"head": lax.rem(h + d, nhead)}, device_id_type=MESH)

    loads = [
        pltpu.make_async_copy(src, dst, in_sem.at[i])
        for i, (src, dst) in enumerate(((k_hbm, k_ref), (v_hbm, v_ref), (q_hbm, q_ref), (g_hbm, g_ref)))
    ]
    for copy in loads:
        copy.start()

    def scatter(phase):
        for p in peers:
            pltpu.make_async_remote_copy(
                snd.at[phase, p, pl.ds(0, piece + 1)], rcv.at[phase, me, pl.ds(0, piece + 1)],
                send_sem.at[phase], recv_sem.at[phase],
                device_id={"ctx": p}, device_id_type=MESH,
            ).start()
        rcv[phase, me] = snd[phase, me]

    def gather_wait(phase):
        part = rcv.at[phase, pl.ds(0, nctx - 1), pl.ds(0, piece + 1)]
        pltpu.make_async_copy(part, part, recv_sem.at[phase]).wait()

    def running(phase, backward):
        def step(i, carry):
            total, tag = carry
            e = nctx - 1 - i if backward else i
            snd[phase + 1, e, pl.ds(0, piece)] = total
            snd[phase + 1, e, pl.ds(piece, 1)] = tag
            own = rcv[phase, e, pl.ds(piece, 1)]
            total = rcv[phase, e, pl.ds(0, piece)] + jnp.where(own == tag, total, 0.0)
            return total, own

        lax.fori_loop(0, nctx, step, (jnp.zeros((piece, HD), F32), jnp.full((1, HD), -1.0, F32)), unroll=8)

    def state(phase, i):
        per = HD // piece
        return rcv[phase, pl.ds(i * per, per), pl.ds(0, piece)].reshape(HD, HD)

    def put_state(phase, i, value):
        per = HD // piece
        snd[phase, pl.ds(i * per, per), pl.ds(0, piece)] = value.reshape(per, piece, HD)

    def head(ref, i):
        return ref[:, pl.ds(i * HD, HD)]

    ids = ids_ref[...].astype(F32)
    col = jnp.broadcast_to(ids, (HD, rows)).T
    first, last = ids[:, 0:1], ids[:, rows - 1 : rows]

    snd[0, :, pl.ds(piece, 1)] = jnp.broadcast_to(last[None], (nctx, 1, HD))
    last_mask = (col == last).astype(F32).astype(BF16)
    loads[0].wait()
    loads[1].wait()
    for i in range(heads):
        put_state(0, i, dot(head(k_ref, i) * last_mask, head(v_ref, i), 0, 0))
    pl.semaphore_wait(barrier, len(peers) + nhead - 1)
    scatter(0)

    wide = jnp.concatenate([col] * (rows // HD), axis=1)
    t = lax.broadcasted_iota(jnp.int32, (rows, rows), 0)
    s = lax.broadcasted_iota(jnp.int32, (rows, rows), 1)
    visible = jnp.where((s <= t) & (wide == ids), 1.0, 0.0)
    loads[2].wait()
    for i in range(heads):
        hi, lo = split(dot(head(q_ref, i), head(k_ref, i), 1, 1) * visible)
        sc_hi[i], sc_lo[i] = hi, lo
        att[:, pl.ds(i * HD, HD)] = dot(hi, head(v_ref, i), 1, 0) + dot(lo, head(v_ref, i), 1, 0)
    loads[3].wait()
    wgt[...] = gain_ref[...] * g_ref[...].astype(F32)

    gather_wait(0)
    running(0, False)
    scatter(1)
    gather_wait(1)

    in_mask = (col == rcv[1, 0, pl.ds(piece, 1)]).astype(F32)
    square = jnp.zeros((rows, HD), F32)
    cross = jnp.zeros((rows, HD), F32)
    for i in range(heads):
        hi, lo = split(state(1, i))
        st_hi[i], st_lo[i] = hi, lo
        a = head(att, i) + in_mask * (dot(head(q_ref, i), hi, 1, 0) + dot(head(q_ref, i), lo, 1, 0))
        att[:, pl.ds(i * HD, HD)] = a
        square += a * a
        cross += a * head(wgt, i)
    ps_snd[0:1, :] = jnp.sum(square.T, axis=0, keepdims=True)
    ps_snd[1:2, :] = jnp.sum(cross.T, axis=0, keepdims=True)
    for d in range(1, nhead):
        pltpu.make_async_remote_copy(
            ps_snd, ps_rcv.at[h], ps_sem.at[0], ps_sem.at[1],
            device_id={"head": lax.rem(h + d, nhead)}, device_id_type=MESH,
        ).start()
    ps_rcv[h] = ps_snd[...]
    part = ps_rcv.at[pl.ds(0, nhead - 1)]
    pltpu.make_async_copy(part, part, ps_sem.at[1]).wait()
    sums = jnp.sum(ps_rcv[...], axis=0)
    inv = lax.rsqrt(sums[0:1] / features + EPSILON)
    back = inv * inv * sums[1:2] / features
    inv = jnp.broadcast_to(inv, (HD, rows)).T
    back = jnp.broadcast_to(back, (HD, rows)).T

    snd[2, :, pl.ds(piece, 1)] = jnp.broadcast_to(first[None], (nctx, 1, HD))
    first_mask = (col == first).astype(F32).astype(BF16)
    for i in range(heads):
        hi, lo = split(inv * (head(wgt, i) - head(att, i) * back))
        gr_hi[i], gr_lo[i] = hi, lo
        q = head(q_ref, i) * first_mask
        put_state(2, i, dot(q, hi, 0, 0) + dot(q, lo, 0, 0))
    scatter(2)

    def local_grads(i):
        ghi, glo = gr_hi[i], gr_lo[i]
        v = head(v_ref, i)
        bhi, blo = split((dot(ghi, v, 1, 1) + dot(glo, v, 1, 1)) * visible)
        shi, slo = st_hi[i], st_lo[i]
        gq = dot(bhi, head(k_ref, i), 1, 0) + dot(blo, head(k_ref, i), 1, 0)
        gq += in_mask * (dot(ghi, shi, 1, 1) + dot(ghi, slo, 1, 1) + dot(glo, shi, 1, 1))
        oq_ref[:, pl.ds(i * HD, HD)] = gq.astype(BF16)
        q = head(q_ref, i)
        lk[:, pl.ds(i * HD, HD)] = dot(bhi, q, 0, 0) + dot(blo, q, 0, 0)
        lv[:, pl.ds(i * HD, HD)] = dot(sc_hi[i], ghi, 0, 0) + dot(sc_hi[i], glo, 0, 0) + dot(sc_lo[i], ghi, 0, 0)

    for i in range(heads):
        local_grads(i)
    out_q = pltpu.make_async_copy(oq_ref, gq_hbm, out_sem.at[0])
    out_q.start()

    gather_wait(2)
    running(2, True)
    scatter(3)
    gather_wait(3)

    out_mask = (col == rcv[3, 0, pl.ds(piece, 1)]).astype(F32)
    for i in range(heads):
        hi, lo = split(state(3, i))
        v, k = head(v_ref, i), head(k_ref, i)
        ok_ref[:, pl.ds(i * HD, HD)] = (head(lk, i) + out_mask * (dot(v, hi, 1, 1) + dot(v, lo, 1, 1))).astype(BF16)
        ov_ref[:, pl.ds(i * HD, HD)] = (head(lv, i) + out_mask * (dot(k, hi, 1, 0) + dot(k, lo, 1, 0))).astype(BF16)
    out_k = pltpu.make_async_copy(ok_ref, gk_hbm, out_sem.at[1])
    out_v = pltpu.make_async_copy(ov_ref, gv_hbm, out_sem.at[2])
    out_k.start()
    out_v.start()

    for phase in range(4):
        part = snd.at[phase, pl.ds(0, nctx - 1), pl.ds(0, piece + 1)]
        pltpu.make_async_copy(part, part, send_sem.at[phase]).wait()
    part = ps_rcv.at[pl.ds(0, nhead - 1)]
    pltpu.make_async_copy(part, part, ps_sem.at[0]).wait()
    out_q.wait()
    out_k.wait()
    out_v.wait()


def solution(mesh):
    nctx, nhead = mesh.shape["ctx"], mesh.shape["head"]

    def on_device(queries, keys, values, out_grad, gain, segment_ids):
        rows, width = queries.shape
        heads = width // HD
        piece = width // nctx
        any_space = pl.BlockSpec(memory_space=pl.ANY)
        vmem = pl.BlockSpec(memory_space=pltpu.VMEM)
        wide = pltpu.VMEM((rows, width), BF16)
        total = pltpu.VMEM((rows, width), F32)
        return pl.pallas_call(
            functools.partial(kernel, nctx, nhead, width * nhead),
            out_shape=[jax.ShapeDtypeStruct((rows, width), BF16)] * 3,
            in_specs=[any_space] * 4 + [vmem] * 2,
            out_specs=[any_space] * 3,
            scratch_shapes=[wide] * 7
            + [
                pltpu.VMEM((4, nctx, piece + 8, HD), F32),
                pltpu.VMEM((4, nctx, piece + 8, HD), F32),
                pltpu.VMEM((2, rows), F32),
                pltpu.VMEM((nhead, 2, rows), F32),
                pltpu.VMEM((heads, rows, rows), BF16),
                pltpu.VMEM((heads, rows, rows), BF16),
                total,
                total,
                pltpu.VMEM((heads, rows, HD), BF16),
                pltpu.VMEM((heads, rows, HD), BF16),
                pltpu.VMEM((heads, HD, HD), BF16),
                pltpu.VMEM((heads, HD, HD), BF16),
                total,
                total,
                pltpu.SemaphoreType.DMA((4,)),
                pltpu.SemaphoreType.DMA((3,)),
                pltpu.SemaphoreType.DMA((4,)),
                pltpu.SemaphoreType.DMA((4,)),
                pltpu.SemaphoreType.DMA((2,)),
            ],
            compiler_params=pltpu.CompilerParams(
                collective_id=0, has_side_effects=True, vmem_limit_bytes=48 * 1024 * 1024
            ),
            name="scan_grads",
        )(queries, keys, values, out_grad, gain.reshape(1, width), segment_ids.reshape(1, rows))

    return jax.shard_map(
        on_device,
        mesh=mesh,
        in_specs=(
            P("ctx", "head"),
            P("ctx", "head"),
            P("ctx", "head"),
            P("ctx", "head"),
            P("head"),
            P("ctx"),
        ),
        out_specs=(P("ctx", "head"), P("ctx", "head"), P("ctx", "head")),
        check_vma=False,
    )
```

```python
import functools
import random

import jax
import jax.numpy as jnp
from jax import lax
from jax.experimental import pallas as pl
from jax.experimental.pallas import tpu as pltpu
from jax.sharding import PartitionSpec as P

HD = 128
EPSILON = 1e-06
RING = 8
MESH = pl.DeviceIdType.MESH
F32 = jnp.float32
BF16 = jnp.bfloat16


def dot(a, b, ca, cb):
    return lax.dot_general(a, b, (((ca,), (cb,)), ((), ())), preferred_element_type=F32)


def split(x):
    hi = x.astype(BF16)
    return hi, (x - hi.astype(F32)).astype(BF16)


def parts(x, axis):
    return jnp.concatenate(split(x), axis=axis)


def twice(x):
    return jnp.concatenate([x, x], axis=1)


def kernel(
    nctx, nhead, features,
    q_hbm, k_hbm, v_hbm, g_hbm, gain_hbm, ids_hbm,
    oq_ref, ok_ref, ov_ref,
    q_ref, k_ref, v_ref, g_ref, gain_ref, ids_ref,
    snd, rcv, ps_snd, ps_rcv, keep_f, keep_b,
    vis_ref, sc_hi, sc_lo, att, wgt, gr, st, lk, lv, q_two, q_turn, k_two, v_two,
    in_sem, send_sem, recv_sem, ps_sem,
):
    rows, width = q_ref.shape
    heads = width // HD
    piece = snd.shape[2] - 8
    per = HD // piece
    nz = nctx // RING
    me = lax.axis_index("ctx")
    z, y = me // RING, me % RING
    h = lax.axis_index("head")
    turn = 1 - 2 * (h % 2)

    offsets = [(dz, dy) for dz in range(nz) for dy in range(RING) if dz or dy]
    random.Random(1).shuffle(offsets)
    offsets.sort(key=lambda o: -(min(o[0], nz - o[0]) + min(o[1], RING - o[1])))
    peers = [
        lax.rem(z + turn * dz + nz, nz) * RING + lax.rem(y + turn * dy + RING, RING) for dz, dy in offsets
    ]

    barrier = pltpu.get_barrier_semaphore()
    for p in peers:
        pl.semaphore_signal(barrier, inc=1, device_id={"ctx": p}, device_id_type=MESH)
    for d in range(1, nhead):
        pl.semaphore_signal(barrier, inc=1, device_id={"head": lax.rem(h + d, nhead)}, device_id_type=MESH)

    pairs = (
        (ids_hbm, ids_ref), (k_hbm, k_ref), (v_hbm, v_ref), (q_hbm, q_ref), (g_hbm, g_ref), (gain_hbm, gain_ref),
    )
    loads = [pltpu.make_async_copy(src, dst, in_sem.at[i]) for i, (src, dst) in enumerate(pairs)]
    for copy in loads:
        copy.start()

    def scatter(phase, size):
        for p in peers:
            pltpu.make_async_remote_copy(
                snd.at[phase, p, pl.ds(0, size)], rcv.at[phase, me, pl.ds(0, size)],
                send_sem.at[phase], recv_sem.at[phase],
                device_id={"ctx": p}, device_id_type=MESH,
            ).start()
        rcv[phase, me, pl.ds(0, size)] = snd[phase, me, pl.ds(0, size)]

    def gather_wait(phase, size):
        part = rcv.at[phase, pl.ds(0, nctx - 1), pl.ds(0, size)]
        pltpu.make_async_copy(part, part, recv_sem.at[phase]).wait()

    def running(phase, keep, backward):
        def step(i, total):
            e = nctx - 1 - i if backward else i
            snd[phase + 1, e, pl.ds(0, piece)] = total
            return rcv[phase, e, pl.ds(0, piece)] + jnp.where(keep[pl.ds(e, 1), :] > 0.0, total, 0.0)

        lax.fori_loop(0, nctx, step, jnp.zeros((piece, HD), F32), unroll=8)

    def state(phase, i):
        return rcv[phase, pl.ds(i * per, per), pl.ds(0, piece)].reshape(HD, HD)

    def put_state(phase, i, value):
        snd[phase, pl.ds(i * per, per), pl.ds(0, piece)] = value.reshape(per, piece, HD)

    def head(ref, i):
        return ref[:, pl.ds(i * HD, HD)]

    loads[0].wait()
    ids = ids_ref[...].astype(F32)
    col = jnp.broadcast_to(ids, (HD, rows)).T
    first, last = ids[:, 0:1], ids[:, rows - 1 : rows]
    lane = lax.broadcasted_iota(jnp.int32, (1, HD), 1)
    tags = jnp.where(lane < HD // 2, first, last)
    snd[0, :, pl.ds(piece, 1)] = jnp.broadcast_to(tags[None], (nctx, 1, HD))
    last_mask = (col == last).astype(F32).astype(BF16)
    loads[1].wait()
    loads[2].wait()
    for i in range(heads):
        put_state(0, i, dot(head(k_ref, i) * last_mask, head(v_ref, i), 0, 0))
    pl.semaphore_wait(barrier, len(peers) + nhead - 1)
    scatter(0, piece + 1)

    wide = jnp.concatenate([col] * (rows // HD), axis=1)
    t = lax.broadcasted_iota(jnp.int32, (rows, rows), 0)
    s = lax.broadcasted_iota(jnp.int32, (rows, rows), 1)
    vis_ref[...] = jnp.where((s <= t) & (wide == ids), 1.0, 0.0)
    first_mask = (col == first).astype(F32).astype(BF16)
    loads[3].wait()
    for i in range(heads):
        v = head(v_ref, i)
        hi, lo = split(dot(head(q_ref, i), head(k_ref, i), 1, 1) * vis_ref[...])
        sc_hi[i], sc_lo[i] = hi, lo
        att[:, pl.ds(i * HD, HD)] = dot(hi, v, 1, 0) + dot(lo, v, 1, 0)
        q_turn[i] = (head(q_ref, i) * first_mask).T
    loads[4].wait()
    loads[5].wait()
    wgt[...] = gain_ref[...] * g_ref[...].astype(F32)

    gather_wait(0, piece + 1)
    tags = rcv[0, :, pl.ds(piece, 1)].reshape(nctx, HD)
    firsts = jnp.broadcast_to(tags[:, 0:1], (nctx, HD))
    lasts = jnp.broadcast_to(tags[:, HD - 1 : HD], (nctx, HD))
    outside = jnp.full((1, HD), -1.0, F32)
    before = jnp.concatenate([outside, lasts[: nctx - 1]], axis=0)
    after = jnp.concatenate([firsts[1:], outside], axis=0)
    keep_f[...] = (lasts == before).astype(F32)
    running(0, keep_f, False)
    scatter(1, piece)

    keep_b[...] = (firsts == after).astype(F32)
    mine = lax.broadcasted_iota(jnp.int32, (nctx, HD), 0) == me
    tag_in = jnp.max(jnp.where(mine, before, -1.0), axis=0, keepdims=True)
    tag_out = jnp.max(jnp.where(mine, after, -1.0), axis=0, keepdims=True)
    in_mask = (col == tag_in).astype(F32)
    in_bf, out_bf = in_mask.astype(BF16), (col == tag_out).astype(F32).astype(BF16)
    for i in range(heads):
        q_two[i] = twice(head(q_ref, i) * in_bf)
        k_two[i] = twice(head(k_ref, i) * out_bf)
        v_two[i] = twice(head(v_ref, i) * out_bf)

    gather_wait(1, piece)
    square = jnp.zeros((rows, HD), F32)
    cross = jnp.zeros((rows, HD), F32)
    for i in range(heads):
        both = parts(state(1, i), 0)
        st[i] = both
        a = head(att, i) + dot(q_two[i], both, 1, 0)
        att[:, pl.ds(i * HD, HD)] = a
        square += a * a
        cross += a * head(wgt, i)
    ones = jnp.ones((16, 2 * HD), BF16)
    ps_snd[0:1, :] = dot(ones, parts(square, 1), 1, 1)[0:1]
    ps_snd[1:2, :] = dot(ones, parts(cross, 1), 1, 1)[0:1]
    for d in range(1, nhead):
        pltpu.make_async_remote_copy(
            ps_snd, ps_rcv.at[h], ps_sem.at[0], ps_sem.at[1],
            device_id={"head": lax.rem(h + d, nhead)}, device_id_type=MESH,
        ).start()
    ps_rcv[h] = ps_snd[...]
    part = ps_rcv.at[pl.ds(0, nhead - 1)]
    pltpu.make_async_copy(part, part, ps_sem.at[1]).wait()
    sums = jnp.sum(ps_rcv[...], axis=0)
    inv = lax.rsqrt(sums[0:1] / features + EPSILON)
    back = inv * inv * sums[1:2] / features

    def thirds(x):
        hi, rest = x.astype(BF16).astype(F32), x
        rest = rest - hi
        mid = rest.astype(BF16).astype(F32)
        return [hi, mid, rest - mid]

    table = jnp.concatenate(thirds(inv) + thirds(back) + [jnp.zeros((10, rows), F32)], axis=0).astype(BF16)
    r = lax.broadcasted_iota(jnp.int32, (16, 2 * HD), 0)
    c = lax.broadcasted_iota(jnp.int32, (16, 2 * HD), 1)
    pick = jnp.where((r < 3) == (c < HD), 1.0, 0.0).astype(BF16)
    columns = dot(table, pick, 0, 0)
    inv, back = columns[:, :HD], columns[:, HD:]

    for i in range(heads):
        both = parts(inv * (head(wgt, i) - head(att, i) * back), 1)
        gr[i] = both
        total = dot(q_turn[i], both, 1, 0)
        put_state(2, i, total[:, :HD] + total[:, HD:])
    scatter(2, piece)

    def local_grads(i):
        ghi, glo = gr[i, :, :HD], gr[i, :, HD:]
        v = head(v_ref, i)
        bhi, blo = split((dot(ghi, v, 1, 1) + dot(glo, v, 1, 1)) * vis_ref[...])
        shi, slo = st[i, :HD], st[i, HD:]
        gq = dot(ghi, shi, 1, 1) + dot(ghi, slo, 1, 1) + dot(glo, shi, 1, 1)
        gq = (col == tag_in).astype(F32) * gq + dot(bhi, head(k_ref, i), 1, 0) + dot(blo, head(k_ref, i), 1, 0)
        oq_ref[:, pl.ds(i * HD, HD)] = gq.astype(BF16)
        q = head(q_ref, i)
        lk[:, pl.ds(i * HD, HD)] = dot(bhi, q, 0, 0) + dot(blo, q, 0, 0)
        lv[:, pl.ds(i * HD, HD)] = dot(sc_hi[i], ghi, 0, 0) + dot(sc_hi[i], glo, 0, 0) + dot(sc_lo[i], ghi, 0, 0)

    for i in range(heads // 2):
        local_grads(i)

    gather_wait(2, piece)
    running(2, keep_b, True)
    scatter(3, piece)
    for i in range(heads // 2, heads):
        local_grads(i)
    gather_wait(3, piece)

    for i in range(heads):
        total = state(3, i)
        ok_ref[:, pl.ds(i * HD, HD)] = (head(lk, i) + dot(v_two[i], parts(total, 1), 1, 1)).astype(BF16)
        ov_ref[:, pl.ds(i * HD, HD)] = (head(lv, i) + dot(k_two[i], parts(total, 0), 1, 0)).astype(BF16)

    for phase, size in enumerate((piece + 1, piece, piece, piece)):
        part = snd.at[phase, pl.ds(0, nctx - 1), pl.ds(0, size)]
        pltpu.make_async_copy(part, part, send_sem.at[phase]).wait()
    part = ps_rcv.at[pl.ds(0, nhead - 1)]
    pltpu.make_async_copy(part, part, ps_sem.at[0]).wait()


def write_out(a_ref, b_ref, c_ref, a_hbm, b_hbm, c_hbm, sem):
    copies = [
        pltpu.make_async_copy(src, dst, sem.at[i])
        for i, (src, dst) in enumerate(((a_ref, a_hbm), (b_ref, b_hbm), (c_ref, c_hbm)))
    ]
    for copy in copies:
        copy.start()
    for copy in copies:
        copy.wait()


def solution(mesh):
    nctx, nhead = mesh.shape["ctx"], mesh.shape["head"]

    def on_device(queries, keys, values, out_grad, gain, segment_ids):
        rows, width = queries.shape
        heads = width // HD
        piece = width // nctx
        hbm = pl.BlockSpec(memory_space=pltpu.HBM)
        vmem = pl.BlockSpec(memory_space=pltpu.VMEM)
        wide = pltpu.VMEM((rows, width), BF16)
        total = pltpu.VMEM((rows, width), F32)
        double = pltpu.VMEM((heads, rows, 2 * HD), BF16)
        arrays = (queries, keys, values, out_grad, gain.reshape(1, width), segment_ids.reshape(1, rows))
        arrays = [pltpu.with_memory_space_constraint(x, pltpu.HBM) for x in arrays]
        grads = pl.pallas_call(
            functools.partial(kernel, nctx, nhead, width * nhead),
            out_shape=[pltpu.VMEM((rows, width), BF16)] * 3,
            in_specs=[hbm] * 6,
            out_specs=[vmem] * 3,
            scratch_shapes=[wide] * 4
            + [
                pltpu.VMEM((1, width), F32),
                pltpu.VMEM((1, rows), jnp.int32),
                pltpu.VMEM((4, nctx, piece + 8, HD), F32),
                pltpu.VMEM((4, nctx, piece + 8, HD), F32),
                pltpu.VMEM((2, rows), F32),
                pltpu.VMEM((nhead, 2, rows), F32),
                pltpu.VMEM((nctx, HD), F32),
                pltpu.VMEM((nctx, HD), F32),
                pltpu.VMEM((rows, rows), F32),
                pltpu.VMEM((heads, rows, rows), BF16),
                pltpu.VMEM((heads, rows, rows), BF16),
                total,
                total,
                double,
                pltpu.VMEM((heads, 2 * HD, HD), BF16),
                total,
                total,
                double,
                pltpu.VMEM((heads, HD, rows), BF16),
                double,
                double,
                pltpu.SemaphoreType.DMA((6,)),
                pltpu.SemaphoreType.DMA((4,)),
                pltpu.SemaphoreType.DMA((4,)),
                pltpu.SemaphoreType.DMA((2,)),
            ],
            compiler_params=pltpu.CompilerParams(
                collective_id=0, has_side_effects=True, vmem_limit_bytes=40 * 1024 * 1024
            ),
            name="scan_grads",
        )(*arrays)
        return pl.pallas_call(
            write_out,
            out_shape=[jax.ShapeDtypeStruct((rows, width), BF16)] * 3,
            in_specs=[pl.BlockSpec(memory_space=pl.ANY)] * 3,
            out_specs=[hbm] * 3,
            scratch_shapes=[pltpu.SemaphoreType.DMA((3,))],
            name="write_out",
        )(*[pltpu.with_memory_space_constraint(x, pltpu.VMEM) for x in grads])

    return jax.shard_map(
        on_device,
        mesh=mesh,
        in_specs=(
            P("ctx", "head"),
            P("ctx", "head"),
            P("ctx", "head"),
            P("ctx", "head"),
            P("head"),
            P("ctx"),
        ),
        out_specs=(P("ctx", "head"), P("ctx", "head"), P("ctx", "head")),
        check_vma=False,
    )
```

```python
import functools
import random

import jax
import jax.numpy as jnp
from jax import lax
from jax.experimental import pallas as pl
from jax.experimental.pallas import tpu as pltpu
from jax.sharding import PartitionSpec as P

HD = 128
EPSILON = 1e-06
RING = 8
EARLY = (0, 1, 7, 8, 2, 6)
MESH = pl.DeviceIdType.MESH
F32 = jnp.float32
BF16 = jnp.bfloat16


def dot(a, b, ca, cb):
    return lax.dot_general(a, b, (((ca,), (cb,)), ((), ())), preferred_element_type=F32)


def split(x):
    hi = x.astype(BF16)
    return hi, (x - hi.astype(F32)).astype(BF16)


def parts(x, axis):
    return jnp.concatenate(split(x), axis=axis)


def twice(x):
    return jnp.concatenate([x, x], axis=1)


def kernel(
    nctx, nhead, features,
    q_hbm, k_hbm, v_hbm, g_hbm, gain_hbm, ids_hbm,
    oq_ref, ok_ref, ov_ref,
    q_ref, k_ref, v_ref, g_ref, gain_ref, ids_ref,
    snd, rcv, ps_snd, ps_rcv, keep_f, keep_b,
    vis_ref, sc_hi, sc_lo, att, wgt, gr, st, lk, lv, q_two, q_turn, k_two, v_two,
    in_sem, send_sem, recv_sem, head_sem, ps_sem,
):
    rows, width = q_ref.shape
    heads = width // HD
    piece = snd.shape[2] - 8
    per = HD // piece
    nz = nctx // RING
    me = lax.axis_index("ctx")
    z, y = me // RING, me % RING
    h = lax.axis_index("head")
    turn = 1 - 2 * (h % 2)

    offsets = [(dz, dy) for dz in range(nz) for dy in range(RING) if dz or dy]
    offsets.sort(key=lambda o: -(min(o[0], nz - o[0]) + min(o[1], RING - o[1])))
    peers = [
        lax.rem(z + turn * dz + nz, nz) * RING + lax.rem(y + turn * dy + RING, RING) for dz, dy in offsets
    ]

    barrier = pltpu.get_barrier_semaphore()
    for p in peers:
        pl.semaphore_signal(barrier, inc=1, device_id={"ctx": p}, device_id_type=MESH)
    for d in range(1, nhead):
        pl.semaphore_signal(barrier, inc=1, device_id={"head": lax.rem(h + d, nhead)}, device_id_type=MESH)

    pairs = (
        (ids_hbm, ids_ref), (k_hbm, k_ref), (v_hbm, v_ref), (q_hbm, q_ref), (g_hbm, g_ref), (gain_hbm, gain_ref),
    )
    loads = [pltpu.make_async_copy(src, dst, in_sem.at[i]) for i, (src, dst) in enumerate(pairs)]
    for copy in loads:
        copy.start()

    near = me // per

    def send(phase, p, size, landed):
        pltpu.make_async_remote_copy(
            snd.at[phase, p, pl.ds(0, size)], rcv.at[phase, me, pl.ds(0, size)],
            send_sem.at[phase], landed, device_id={"ctx": p}, device_id_type=MESH,
        ).start()

    def keep_own(phase, size, landed):
        pltpu.make_async_copy(snd.at[phase, me, pl.ds(0, size)], rcv.at[phase, me, pl.ds(0, size)], landed).start()

    def scatter(phase, size, landed):
        for p in peers:
            send(phase, p, size, landed)
        keep_own(phase, size, landed)

    def gather_wait(phase, size):
        part = rcv.at[phase, :, pl.ds(0, size)]
        pltpu.make_async_copy(part, part, recv_sem.at[phase]).wait()

    def head_wait(phase, i):
        part = rcv.at[phase, pl.ds(i * per, per), pl.ds(0, piece)]
        pltpu.make_async_copy(part, part, head_sem.at[phase, i]).wait()

    near_first = [lax.rem(near + d, heads) for d in sorted(range(heads), key=lambda d: min(d, heads - d))]

    def running(phase, keep, backward):
        def step(i, total):
            e = nctx - 1 - i if backward else i
            snd[phase + 1, e, pl.ds(0, piece)] = total
            return rcv[phase, e, pl.ds(0, piece)] + jnp.where(keep[pl.ds(e, 1), :] > 0.0, total, 0.0)

        lax.fori_loop(0, nctx, step, jnp.zeros((piece, HD), F32), unroll=8)

    def state(phase, i):
        return rcv[phase, pl.ds(i * per, per), pl.ds(0, piece)].reshape(HD, HD)

    def put_state(phase, i, value):
        snd[phase, pl.ds(i * per, per), pl.ds(0, piece)] = value.reshape(per, piece, HD)

    def head(ref, i):
        return ref[:, pl.ds(i * HD, HD)]

    loads[0].wait()
    ids = ids_ref[...].astype(F32)
    col = jnp.broadcast_to(ids, (HD, rows)).T
    first, last = ids[:, 0:1], ids[:, rows - 1 : rows]
    lane = lax.broadcasted_iota(jnp.int32, (1, HD), 1)
    tags = jnp.where(lane < HD // 2, first, last)
    snd[0, :, pl.ds(piece, 1)] = jnp.broadcast_to(tags[None], (nctx, 1, HD))
    last_mask = (col == last).astype(F32).astype(BF16)
    loads[1].wait()
    loads[2].wait()
    for i in range(heads):
        put_state(0, i, dot(head(k_ref, i) * last_mask, head(v_ref, i), 0, 0))
    pl.semaphore_wait(barrier, len(peers) + nhead - 1)
    scatter(0, piece + 1, recv_sem.at[0])

    wide = jnp.concatenate([col] * (rows // HD), axis=1)
    t = lax.broadcasted_iota(jnp.int32, (rows, rows), 0)
    s = lax.broadcasted_iota(jnp.int32, (rows, rows), 1)
    vis_ref[...] = jnp.where((s <= t) & (wide == ids), 1.0, 0.0)
    first_mask = (col == first).astype(F32).astype(BF16)
    loads[3].wait()
    for i in range(heads):
        v = head(v_ref, i)
        hi, lo = split(dot(head(q_ref, i), head(k_ref, i), 1, 1) * vis_ref[...])
        sc_hi[i], sc_lo[i] = hi, lo
        att[i] = dot(hi, v, 1, 0) + dot(lo, v, 1, 0)
        q_turn[i] = (head(q_ref, i) * first_mask).T
    loads[4].wait()
    loads[5].wait()
    for i in range(heads):
        wgt[i] = head(gain_ref, i) * head(g_ref, i).astype(F32)

    gather_wait(0, piece + 1)
    tags = rcv[0, :, pl.ds(piece, 1)].reshape(nctx, HD)
    firsts = jnp.broadcast_to(tags[:, 0:1], (nctx, HD))
    lasts = jnp.broadcast_to(tags[:, HD - 1 : HD], (nctx, HD))
    outside = jnp.full((1, HD), -1.0, F32)
    before = jnp.concatenate([outside, lasts[: nctx - 1]], axis=0)
    after = jnp.concatenate([firsts[1:], outside], axis=0)
    keep_f[...] = (lasts == before).astype(F32)
    running(0, keep_f, False)
    scatter(1, piece, head_sem.at[1, near])

    keep_b[...] = (firsts == after).astype(F32)
    mine = lax.broadcasted_iota(jnp.int32, (nctx, HD), 0) == me
    tag_in = jnp.max(jnp.where(mine, before, -1.0), axis=0, keepdims=True)
    tag_out = jnp.max(jnp.where(mine, after, -1.0), axis=0, keepdims=True)
    in_mask = (col == tag_in).astype(F32)
    in_bf, out_bf = in_mask.astype(BF16), (col == tag_out).astype(F32).astype(BF16)
    for i in range(heads):
        q_two[i] = twice(head(q_ref, i) * in_bf)
        k_two[i] = twice(head(k_ref, i) * out_bf)
        v_two[i] = twice(head(v_ref, i) * out_bf)

    square = jnp.zeros((rows, HD), F32)
    cross = jnp.zeros((rows, HD), F32)
    for i in near_first:
        head_wait(1, i)
        both = parts(state(1, i), 0)
        st[i] = both
        a = att[i] + dot(q_two[i], both, 1, 0)
        att[i] = a
        square += a * a
        cross += a * wgt[i]
    ones = jnp.ones((16, 2 * HD), BF16)
    ps_snd[0:1, :] = dot(ones, parts(square, 1), 1, 1)[0:1]
    ps_snd[1:2, :] = dot(ones, parts(cross, 1), 1, 1)[0:1]
    for d in range(1, nhead):
        pltpu.make_async_remote_copy(
            ps_snd, ps_rcv.at[h], ps_sem.at[0], ps_sem.at[1],
            device_id={"head": lax.rem(h + d, nhead)}, device_id_type=MESH,
        ).start()
    ps_rcv[h] = ps_snd[...]
    part = ps_rcv.at[pl.ds(0, nhead - 1)]
    pltpu.make_async_copy(part, part, ps_sem.at[1]).wait()
    sums = jnp.sum(ps_rcv[...], axis=0)
    inv = lax.rsqrt(sums[0:1] / features + EPSILON)
    back = inv * inv * sums[1:2] / features

    def thirds(x):
        hi, rest = x.astype(BF16).astype(F32), x
        rest = rest - hi
        mid = rest.astype(BF16).astype(F32)
        return [hi, mid, rest - mid]

    table = jnp.concatenate(thirds(inv) + thirds(back) + [jnp.zeros((10, rows), F32)], axis=0).astype(BF16)
    r = lax.broadcasted_iota(jnp.int32, (16, 2 * HD), 0)
    c = lax.broadcasted_iota(jnp.int32, (16, 2 * HD), 1)
    pick = jnp.where((r < 3) == (c < HD), 1.0, 0.0).astype(BF16)
    columns = dot(table, pick, 0, 0)
    inv, back = columns[:, :HD], columns[:, HD:]

    for i in reversed(near_first):
        both = parts(inv * (wgt[i] - att[i] * back), 1)
        gr[i] = both
        total = dot(q_turn[i], both, 1, 0)
        put_state(2, i, total[:, :HD] + total[:, HD:])
    scatter(2, piece, recv_sem.at[2])

    def local_grads(i):
        ghi, glo = gr[i, :, :HD], gr[i, :, HD:]
        v = head(v_ref, i)
        bhi, blo = split((dot(ghi, v, 1, 1) + dot(glo, v, 1, 1)) * vis_ref[...])
        shi, slo = st[i, :HD], st[i, HD:]
        gq = dot(ghi, shi, 1, 1) + dot(ghi, slo, 1, 1) + dot(glo, shi, 1, 1)
        gq = (col == tag_in).astype(F32) * gq + dot(bhi, head(k_ref, i), 1, 0) + dot(blo, head(k_ref, i), 1, 0)
        oq_ref[:, pl.ds(i * HD, HD)] = gq.astype(BF16)
        q = head(q_ref, i)
        lk[i] = dot(bhi, q, 0, 0) + dot(blo, q, 0, 0)
        lv[i] = dot(sc_hi[i], ghi, 0, 0) + dot(sc_hi[i], glo, 0, 0) + dot(sc_lo[i], ghi, 0, 0)

    for i in range(heads // 2):
        local_grads(i)

    gather_wait(2, piece)
    running(2, keep_b, True)
    for p in EARLY:
        pl.when(me != p)(functools.partial(send, 3, p, piece, head_sem.at[3, near]))
    for p in peers:
        others = functools.reduce(lambda a, b: a & b, [p != f for f in EARLY])
        pl.when(others)(functools.partial(send, 3, p, piece, head_sem.at[3, near]))
    keep_own(3, piece, head_sem.at[3, near])
    for i in range(heads // 2, heads):
        local_grads(i)
    for i in near_first:
        head_wait(3, i)
        total = state(3, i)
        at = pl.ds(pl.multiple_of(i * HD, HD), HD)
        ok_ref[:, at] = (lk[i] + dot(v_two[i], parts(total, 1), 1, 1)).astype(BF16)
        ov_ref[:, at] = (lv[i] + dot(k_two[i], parts(total, 0), 1, 0)).astype(BF16)

    for phase, size in enumerate((piece + 1, piece, piece, piece)):
        part = snd.at[phase, pl.ds(0, nctx - 1), pl.ds(0, size)]
        pltpu.make_async_copy(part, part, send_sem.at[phase]).wait()
    part = ps_rcv.at[pl.ds(0, nhead - 1)]
    pltpu.make_async_copy(part, part, ps_sem.at[0]).wait()


def write_out(a_ref, b_ref, c_ref, a_hbm, b_hbm, c_hbm, sem):
    copies = [
        pltpu.make_async_copy(src, dst, sem.at[i])
        for i, (src, dst) in enumerate(((a_ref, a_hbm), (b_ref, b_hbm), (c_ref, c_hbm)))
    ]
    for copy in copies:
        copy.start()
    for copy in copies:
        copy.wait()


def solution(mesh):
    nctx, nhead = mesh.shape["ctx"], mesh.shape["head"]

    def on_device(queries, keys, values, out_grad, gain, segment_ids):
        rows, width = queries.shape
        heads = width // HD
        piece = width // nctx
        hbm = pl.BlockSpec(memory_space=pltpu.HBM)
        vmem = pl.BlockSpec(memory_space=pltpu.VMEM)
        wide = pltpu.VMEM((rows, width), BF16)
        total = pltpu.VMEM((heads, rows, HD), F32)
        double = pltpu.VMEM((heads, rows, 2 * HD), BF16)
        arrays = (queries, keys, values, out_grad, gain.reshape(1, width), segment_ids.reshape(1, rows))
        arrays = [pltpu.with_memory_space_constraint(x, pltpu.HBM) for x in arrays]
        grads = pl.pallas_call(
            functools.partial(kernel, nctx, nhead, width * nhead),
            out_shape=[pltpu.VMEM((rows, width), BF16)] * 3,
            in_specs=[hbm] * 6,
            out_specs=[vmem] * 3,
            scratch_shapes=[wide] * 4
            + [
                pltpu.VMEM((1, width), F32),
                pltpu.VMEM((1, rows), jnp.int32),
                pltpu.VMEM((4, nctx, piece + 8, HD), F32),
                pltpu.VMEM((4, nctx, piece + 8, HD), F32),
                pltpu.VMEM((2, rows), F32),
                pltpu.VMEM((nhead, 2, rows), F32),
                pltpu.VMEM((nctx, HD), F32),
                pltpu.VMEM((nctx, HD), F32),
                pltpu.VMEM((rows, rows), F32),
                pltpu.VMEM((heads, rows, rows), BF16),
                pltpu.VMEM((heads, rows, rows), BF16),
                total,
                total,
                double,
                pltpu.VMEM((heads, 2 * HD, HD), BF16),
                total,
                total,
                double,
                pltpu.VMEM((heads, HD, rows), BF16),
                double,
                double,
                pltpu.SemaphoreType.DMA((6,)),
                pltpu.SemaphoreType.DMA((4,)),
                pltpu.SemaphoreType.DMA((4,)),
                pltpu.SemaphoreType.DMA((4, heads)),
                pltpu.SemaphoreType.DMA((2,)),
            ],
            compiler_params=pltpu.CompilerParams(
                collective_id=0, has_side_effects=True, vmem_limit_bytes=40 * 1024 * 1024
            ),
            name="scan_grads",
        )(*arrays)
        return pl.pallas_call(
            write_out,
            out_shape=[jax.ShapeDtypeStruct((rows, width), BF16)] * 3,
            in_specs=[pl.BlockSpec(memory_space=pl.ANY)] * 3,
            out_specs=[hbm] * 3,
            scratch_shapes=[pltpu.SemaphoreType.DMA((3,))],
            name="write_out",
        )(*[pltpu.with_memory_space_constraint(x, pltpu.VMEM) for x in grads])

    return jax.shard_map(
        on_device,
        mesh=mesh,
        in_specs=(
            P("ctx", "head"),
            P("ctx", "head"),
            P("ctx", "head"),
            P("ctx", "head"),
            P("head"),
            P("ctx"),
        ),
        out_specs=(P("ctx", "head"), P("ctx", "head"), P("ctx", "head")),
        check_vma=False,
    )
```

```python
import functools
import random

import jax
import jax.numpy as jnp
from jax import lax
from jax.experimental import pallas as pl
from jax.experimental.pallas import tpu as pltpu
from jax.sharding import PartitionSpec as P

HD = 128
EPSILON = 1e-06
RING = 8
EARLY = (0, 1, 7, 8, 2, 6)
MESH = pl.DeviceIdType.MESH
F32 = jnp.float32
BF16 = jnp.bfloat16


def dot(a, b, ca, cb):
    return lax.dot_general(a, b, (((ca,), (cb,)), ((), ())), preferred_element_type=F32)


def split(x):
    hi = x.astype(BF16)
    return hi, (x - hi.astype(F32)).astype(BF16)


def parts(x, axis):
    return jnp.concatenate(split(x), axis=axis)


def twice(x):
    return jnp.concatenate([x, x], axis=1)


def kernel(
    nctx, nhead, features,
    q_hbm, k_hbm, v_hbm, g_hbm, gain_hbm, ids_hbm,
    oq_ref, ok_ref, ov_ref,
    q_ref, k_ref, v_ref, g_ref, gain_ref, ids_ref,
    snd, rcv, ps_snd, ps_rcv, keep_f, keep_b,
    vis_ref, sc_hi, sc_lo, att, wgt, gr, st, lk, lv, q_two, q_turn, k_two, v_two,
    in_sem, send_sem, recv_sem, head_sem, ps_sem,
):
    rows, width = q_ref.shape
    heads = width // HD
    piece = snd.shape[2] - 8
    per = HD // piece
    nz = nctx // RING
    me = lax.axis_index("ctx")
    z, y = me // RING, me % RING
    h = lax.axis_index("head")
    turn = 1 - 2 * (h % 2)

    offsets = [(dz, dy) for dz in range(nz) for dy in range(RING) if dz or dy]
    offsets.sort(key=lambda o: -(min(o[0], nz - o[0]) + min(o[1], RING - o[1])))
    peers = [
        lax.rem(z + turn * dz + nz, nz) * RING + lax.rem(y + turn * dy + RING, RING) for dz, dy in offsets
    ]

    barrier = pltpu.get_barrier_semaphore()
    for p in peers:
        pl.semaphore_signal(barrier, inc=1, device_id={"ctx": p}, device_id_type=MESH)
    for d in range(1, nhead):
        pl.semaphore_signal(barrier, inc=1, device_id={"head": lax.rem(h + d, nhead)}, device_id_type=MESH)

    pairs = (
        (ids_hbm, ids_ref), (k_hbm, k_ref), (v_hbm, v_ref), (q_hbm, q_ref), (g_hbm, g_ref), (gain_hbm, gain_ref),
    )
    loads = [pltpu.make_async_copy(src, dst, in_sem.at[i]) for i, (src, dst) in enumerate(pairs)]
    for copy in loads:
        copy.start()

    near = me // per

    def send(phase, p, size, landed):
        pltpu.make_async_remote_copy(
            snd.at[phase, p, pl.ds(0, size)], rcv.at[phase, me, pl.ds(0, size)],
            send_sem.at[phase], landed, device_id={"ctx": p}, device_id_type=MESH,
        ).start()

    def keep_own(phase, size, landed):
        pltpu.make_async_copy(snd.at[phase, me, pl.ds(0, size)], rcv.at[phase, me, pl.ds(0, size)], landed).start()

    def scatter(phase, size, landed):
        for p in peers:
            send(phase, p, size, landed)
        keep_own(phase, size, landed)

    def gather_wait(phase, size):
        part = rcv.at[phase, :, pl.ds(0, size)]
        pltpu.make_async_copy(part, part, recv_sem.at[phase]).wait()

    def head_wait(phase, i):
        part = rcv.at[phase, pl.ds(i * per, per), pl.ds(0, piece)]
        pltpu.make_async_copy(part, part, head_sem.at[phase, i]).wait()

    near_first = [lax.rem(near + d, heads) for d in sorted(range(heads), key=lambda d: min(d, heads - d))]

    def running(phase, keep, backward):
        def step(i, total):
            e = nctx - 1 - i if backward else i
            snd[phase + 1, e, pl.ds(0, piece)] = total
            return rcv[phase, e, pl.ds(0, piece)] + jnp.where(keep[pl.ds(e, 1), :] > 0.0, total, 0.0)

        lax.fori_loop(0, nctx, step, jnp.zeros((piece, HD), F32), unroll=8)

    def state(phase, i):
        return rcv[phase, pl.ds(i * per, per), pl.ds(0, piece)].reshape(HD, HD)

    def put_state(phase, i, value):
        snd[phase, pl.ds(i * per, per), pl.ds(0, piece)] = value.reshape(per, piece, HD)

    def head(ref, i):
        return ref[:, pl.ds(i * HD, HD)]

    loads[0].wait()
    ids = ids_ref[...].astype(F32)
    col = jnp.broadcast_to(ids, (HD, rows)).T
    first, last = ids[:, 0:1], ids[:, rows - 1 : rows]
    lane = lax.broadcasted_iota(jnp.int32, (1, HD), 1)
    tags = jnp.where(lane < HD // 2, first, last)
    snd[0, :, pl.ds(piece, 1)] = jnp.broadcast_to(tags[None], (nctx, 1, HD))
    last_mask = (col == last).astype(F32).astype(BF16)
    loads[1].wait()
    loads[2].wait()
    for i in range(heads):
        put_state(0, i, dot(head(k_ref, i) * last_mask, head(v_ref, i), 0, 0))
    pl.semaphore_wait(barrier, len(peers) + nhead - 1)
    scatter(0, piece + 1, recv_sem.at[0])

    wide = jnp.concatenate([col] * (rows // HD), axis=1)
    t = lax.broadcasted_iota(jnp.int32, (rows, rows), 0)
    s = lax.broadcasted_iota(jnp.int32, (rows, rows), 1)
    vis_ref[...] = jnp.where((s <= t) & (wide == ids), 1.0, 0.0)
    first_mask = (col == first).astype(F32).astype(BF16)
    loads[3].wait()
    for i in range(heads):
        v = head(v_ref, i)
        hi, lo = split(dot(head(q_ref, i), head(k_ref, i), 1, 1) * vis_ref[...])
        sc_hi[i], sc_lo[i] = hi, lo
        att[i] = (dot(hi, v, 1, 0) + dot(lo, v, 1, 0)).T
        q_turn[i] = (head(q_ref, i) * first_mask).T
    loads[4].wait()
    loads[5].wait()
    for i in range(heads):
        wgt[i] = (head(gain_ref, i) * head(g_ref, i).astype(F32)).T

    gather_wait(0, piece + 1)
    tags = rcv[0, :, pl.ds(piece, 1)].reshape(nctx, HD)
    firsts = jnp.broadcast_to(tags[:, 0:1], (nctx, HD))
    lasts = jnp.broadcast_to(tags[:, HD - 1 : HD], (nctx, HD))
    outside = jnp.full((1, HD), -1.0, F32)
    before = jnp.concatenate([outside, lasts[: nctx - 1]], axis=0)
    after = jnp.concatenate([firsts[1:], outside], axis=0)
    keep_f[...] = (lasts == before).astype(F32)
    running(0, keep_f, False)
    scatter(1, piece, head_sem.at[1, near])

    keep_b[...] = (firsts == after).astype(F32)
    mine = lax.broadcasted_iota(jnp.int32, (nctx, HD), 0) == me
    tag_in = jnp.max(jnp.where(mine, before, -1.0), axis=0, keepdims=True)
    tag_out = jnp.max(jnp.where(mine, after, -1.0), axis=0, keepdims=True)
    in_mask = (col == tag_in).astype(F32)
    in_bf, out_bf = in_mask.astype(BF16), (col == tag_out).astype(F32).astype(BF16)
    for i in range(heads):
        q_two[i] = twice(head(q_ref, i) * in_bf)
        k_two[i] = twice(head(k_ref, i) * out_bf)
        v_two[i] = twice(head(v_ref, i) * out_bf)

    square = jnp.zeros((HD, rows), F32)
    cross = jnp.zeros((HD, rows), F32)
    for i in near_first:
        head_wait(1, i)
        both = parts(state(1, i).T, 1)
        st[i] = both
        a = att[i] + dot(both, q_two[i], 1, 1)
        att[i] = a
        square += a * a
        cross += a * wgt[i]
    ps_snd[0:1, :] = jnp.sum(square, axis=0, keepdims=True)
    ps_snd[1:2, :] = jnp.sum(cross, axis=0, keepdims=True)
    for d in range(1, nhead):
        pltpu.make_async_remote_copy(
            ps_snd, ps_rcv.at[h], ps_sem.at[0], ps_sem.at[1],
            device_id={"head": lax.rem(h + d, nhead)}, device_id_type=MESH,
        ).start()
    ps_rcv[h] = ps_snd[...]
    part = ps_rcv.at[pl.ds(0, nhead - 1)]
    pltpu.make_async_copy(part, part, ps_sem.at[1]).wait()
    sums = jnp.sum(ps_rcv[...], axis=0)
    inv = lax.rsqrt(sums[0:1] / features + EPSILON)
    back = inv * inv * sums[1:2] / features

    rows_of = per // RING
    for i in reversed(near_first):
        both = parts(inv * (wgt[i] - att[i] * back), 0)
        gr[i] = both
        total = dot(q_turn[i], both, 1, 1)
        put_state(2, i, total[:, :HD] + total[:, HD:])
        for dy in sorted(range(RING), key=lambda d: -min(d, RING - d)):
            py = lax.rem(y + turn * dy + RING, RING)
            for r in range(rows_of):
                p = (i * rows_of + lax.rem(z + r, rows_of)) * RING + py
                if i is near_first[0] and dy == 0 and r == 0:
                    keep_own(2, piece, recv_sem.at[2])
                else:
                    send(2, p, piece, recv_sem.at[2])

    def local_grads(i):
        ghi, glo = gr[i, :HD].T, gr[i, HD:].T
        v = head(v_ref, i)
        bhi, blo = split((dot(ghi, v, 1, 1) + dot(glo, v, 1, 1)) * vis_ref[...])
        shi, slo = st[i, :, :HD], st[i, :, HD:]
        gq = dot(ghi, shi, 1, 0) + dot(ghi, slo, 1, 0) + dot(glo, shi, 1, 0)
        gq = (col == tag_in).astype(F32) * gq + dot(bhi, head(k_ref, i), 1, 0) + dot(blo, head(k_ref, i), 1, 0)
        oq_ref[:, pl.ds(i * HD, HD)] = gq.astype(BF16)
        q = head(q_ref, i)
        lk[i] = dot(bhi, q, 0, 0) + dot(blo, q, 0, 0)
        lv[i] = dot(sc_hi[i], ghi, 0, 0) + dot(sc_hi[i], glo, 0, 0) + dot(sc_lo[i], ghi, 0, 0)

    for i in range(heads // 2):
        local_grads(i)

    gather_wait(2, piece)
    running(2, keep_b, True)
    for p in EARLY:
        pl.when(me != p)(functools.partial(send, 3, p, piece, head_sem.at[3, near]))
    for p in peers:
        others = functools.reduce(lambda a, b: a & b, [p != f for f in EARLY])
        pl.when(others)(functools.partial(send, 3, p, piece, head_sem.at[3, near]))
    keep_own(3, piece, head_sem.at[3, near])
    for i in range(heads // 2, heads):
        local_grads(i)
    for i in near_first:
        head_wait(3, i)
        total = state(3, i)
        at = pl.ds(pl.multiple_of(i * HD, HD), HD)
        ok_ref[:, at] = (lk[i] + dot(v_two[i], parts(total, 1), 1, 1)).astype(BF16)
        ov_ref[:, at] = (lv[i] + dot(k_two[i], parts(total, 0), 1, 0)).astype(BF16)

    for phase, size in enumerate((piece + 1, piece, piece, piece)):
        part = snd.at[phase, pl.ds(0, nctx - 1), pl.ds(0, size)]
        pltpu.make_async_copy(part, part, send_sem.at[phase]).wait()
    part = ps_rcv.at[pl.ds(0, nhead - 1)]
    pltpu.make_async_copy(part, part, ps_sem.at[0]).wait()


def write_out(a_ref, b_ref, c_ref, a_hbm, b_hbm, c_hbm, sem):
    copies = [
        pltpu.make_async_copy(src, dst, sem.at[i])
        for i, (src, dst) in enumerate(((a_ref, a_hbm), (b_ref, b_hbm), (c_ref, c_hbm)))
    ]
    for copy in copies:
        copy.start()
    for copy in copies:
        copy.wait()


def solution(mesh):
    nctx, nhead = mesh.shape["ctx"], mesh.shape["head"]

    def on_device(queries, keys, values, out_grad, gain, segment_ids):
        rows, width = queries.shape
        heads = width // HD
        piece = width // nctx
        hbm = pl.BlockSpec(memory_space=pltpu.HBM)
        vmem = pl.BlockSpec(memory_space=pltpu.VMEM)
        wide = pltpu.VMEM((rows, width), BF16)
        total = pltpu.VMEM((heads, rows, HD), F32)
        turned = pltpu.VMEM((heads, HD, rows), F32)
        double = pltpu.VMEM((heads, rows, 2 * HD), BF16)
        arrays = (queries, keys, values, out_grad, gain.reshape(1, width), segment_ids.reshape(1, rows))
        arrays = [pltpu.with_memory_space_constraint(x, pltpu.HBM) for x in arrays]
        grads = pl.pallas_call(
            functools.partial(kernel, nctx, nhead, width * nhead),
            out_shape=[pltpu.VMEM((rows, width), BF16)] * 3,
            in_specs=[hbm] * 6,
            out_specs=[vmem] * 3,
            scratch_shapes=[wide] * 4
            + [
                pltpu.VMEM((1, width), F32),
                pltpu.VMEM((1, rows), jnp.int32),
                pltpu.VMEM((4, nctx, piece + 8, HD), F32),
                pltpu.VMEM((4, nctx, piece + 8, HD), F32),
                pltpu.VMEM((2, rows), F32),
                pltpu.VMEM((nhead, 2, rows), F32),
                pltpu.VMEM((nctx, HD), F32),
                pltpu.VMEM((nctx, HD), F32),
                pltpu.VMEM((rows, rows), F32),
                pltpu.VMEM((heads, rows, rows), BF16),
                pltpu.VMEM((heads, rows, rows), BF16),
                turned,
                turned,
                pltpu.VMEM((heads, 2 * HD, rows), BF16),
                pltpu.VMEM((heads, HD, 2 * HD), BF16),
                total,
                total,
                double,
                pltpu.VMEM((heads, HD, rows), BF16),
                double,
                double,
                pltpu.SemaphoreType.DMA((6,)),
                pltpu.SemaphoreType.DMA((4,)),
                pltpu.SemaphoreType.DMA((4,)),
                pltpu.SemaphoreType.DMA((4, heads)),
                pltpu.SemaphoreType.DMA((2,)),
            ],
            compiler_params=pltpu.CompilerParams(
                collective_id=0, has_side_effects=True, vmem_limit_bytes=40 * 1024 * 1024
            ),
            name="scan_grads",
        )(*arrays)
        return pl.pallas_call(
            write_out,
            out_shape=[jax.ShapeDtypeStruct((rows, width), BF16)] * 3,
            in_specs=[pl.BlockSpec(memory_space=pl.ANY)] * 3,
            out_specs=[hbm] * 3,
            scratch_shapes=[pltpu.SemaphoreType.DMA((3,))],
            name="write_out",
        )(*[pltpu.with_memory_space_constraint(x, pltpu.VMEM) for x in grads])

    return jax.shard_map(
        on_device,
        mesh=mesh,
        in_specs=(
            P("ctx", "head"),
            P("ctx", "head"),
            P("ctx", "head"),
            P("ctx", "head"),
            P("head"),
            P("ctx"),
        ),
        out_specs=(P("ctx", "head"), P("ctx", "head"), P("ctx", "head")),
        check_vma=False,
    )
```

```python
import functools
import random

import jax
import jax.numpy as jnp
from jax import lax
from jax.experimental import pallas as pl
from jax.experimental.pallas import tpu as pltpu
from jax.sharding import PartitionSpec as P

HD = 128
EPSILON = 1e-06
RING = 8
EARLY = (1, 2, 9, 0, 8, 7, 10, 3)
MESH = pl.DeviceIdType.MESH
F32 = jnp.float32
BF16 = jnp.bfloat16


def dot(a, b, ca, cb):
    return lax.dot_general(a, b, (((ca,), (cb,)), ((), ())), preferred_element_type=F32)


def split(x):
    hi = x.astype(BF16)
    return hi, (x - hi.astype(F32)).astype(BF16)


def parts(x, axis):
    return jnp.concatenate(split(x), axis=axis)


def twice(x):
    return jnp.concatenate([x, x], axis=1)


def kernel(
    nctx, nhead, features,
    q_hbm, k_hbm, v_hbm, g_hbm, gain_hbm, ids_hbm,
    oq_ref, ok_ref, ov_ref,
    q_ref, k_ref, v_ref, g_ref, gain_ref, ids_ref,
    snd, rcv, ps_snd, ps_rcv, keep_f, keep_b,
    vis_ref, sc_hi, sc_lo, att, wgt, gr, st, lk, lv, q_two, q_turn, k_two, v_two,
    in_sem, send_sem, recv_sem, head_sem, ps_sem,
):
    rows, width = q_ref.shape
    heads = width // HD
    piece = snd.shape[2] - 8
    per = HD // piece
    nz = nctx // RING
    me = lax.axis_index("ctx")
    z, y = me // RING, me % RING
    h = lax.axis_index("head")
    turn = 1 - 2 * (h % 2)

    offsets = [(dz, dy) for dz in range(nz) for dy in range(RING) if dz or dy]
    offsets.sort(key=lambda o: -(min(o[0], nz - o[0]) + min(o[1], RING - o[1])))
    peers = [
        lax.rem(z + turn * dz + nz, nz) * RING + lax.rem(y + turn * dy + RING, RING) for dz, dy in offsets
    ]

    barrier = pltpu.get_barrier_semaphore()
    for p in peers:
        pl.semaphore_signal(barrier, inc=1, device_id={"ctx": p}, device_id_type=MESH)
    for d in range(1, nhead):
        pl.semaphore_signal(barrier, inc=1, device_id={"head": lax.rem(h + d, nhead)}, device_id_type=MESH)

    pairs = (
        (ids_hbm, ids_ref), (k_hbm, k_ref), (v_hbm, v_ref), (q_hbm, q_ref), (g_hbm, g_ref), (gain_hbm, gain_ref),
    )
    loads = [pltpu.make_async_copy(src, dst, in_sem.at[i]) for i, (src, dst) in enumerate(pairs)]
    for copy in loads:
        copy.start()

    near = me // per

    def send(phase, p, size, landed):
        pltpu.make_async_remote_copy(
            snd.at[phase, p, pl.ds(0, size)], rcv.at[phase, me, pl.ds(0, size)],
            send_sem.at[phase], landed, device_id={"ctx": p}, device_id_type=MESH,
        ).start()

    def keep_own(phase, size, landed):
        pltpu.make_async_copy(snd.at[phase, me, pl.ds(0, size)], rcv.at[phase, me, pl.ds(0, size)], landed).start()

    def scatter(phase, size, landed):
        for p in peers:
            send(phase, p, size, landed)
        keep_own(phase, size, landed)

    def gather_wait(phase, size):
        part = rcv.at[phase, :, pl.ds(0, size)]
        pltpu.make_async_copy(part, part, recv_sem.at[phase]).wait()

    def head_wait(phase, i):
        part = rcv.at[phase, pl.ds(i * per, per), pl.ds(0, piece)]
        pltpu.make_async_copy(part, part, head_sem.at[phase, i]).wait()

    near_first = [lax.rem(near + d, heads) for d in sorted(range(heads), key=lambda d: min(d, heads - d))]

    def running(phase, keep, backward):
        def step(i, total):
            e = nctx - 1 - i if backward else i
            snd[phase + 1, e, pl.ds(0, piece)] = total
            return rcv[phase, e, pl.ds(0, piece)] + jnp.where(keep[pl.ds(e, 1), :] > 0.0, total, 0.0)

        lax.fori_loop(0, nctx, step, jnp.zeros((piece, HD), F32), unroll=8)

    def state(phase, i):
        return rcv[phase, pl.ds(i * per, per), pl.ds(0, piece)].reshape(HD, HD)

    def put_state(phase, i, value):
        snd[phase, pl.ds(i * per, per), pl.ds(0, piece)] = value.reshape(per, piece, HD)

    def head(ref, i):
        return ref[:, pl.ds(i * HD, HD)]

    loads[0].wait()
    ids = ids_ref[...].astype(F32)
    col = jnp.broadcast_to(ids, (HD, rows)).T
    first, last = ids[:, 0:1], ids[:, rows - 1 : rows]
    lane = lax.broadcasted_iota(jnp.int32, (1, HD), 1)
    tags = jnp.where(lane < HD // 2, first, last)
    snd[0, :, pl.ds(piece, 1)] = jnp.broadcast_to(tags[None], (nctx, 1, HD))
    last_mask = (col == last).astype(F32).astype(BF16)
    loads[1].wait()
    loads[2].wait()
    for i in range(heads):
        put_state(0, i, dot(head(k_ref, i) * last_mask, head(v_ref, i), 0, 0))
    pl.semaphore_wait(barrier, len(peers) + nhead - 1)
    scatter(0, piece + 1, recv_sem.at[0])

    wide = jnp.concatenate([col] * (rows // HD), axis=1)
    t = lax.broadcasted_iota(jnp.int32, (rows, rows), 0)
    s = lax.broadcasted_iota(jnp.int32, (rows, rows), 1)
    vis_ref[...] = jnp.where((s <= t) & (wide == ids), 1.0, 0.0)
    first_mask = (col == first).astype(F32).astype(BF16)
    loads[3].wait()
    for i in range(heads):
        v = head(v_ref, i)
        hi, lo = split(dot(head(q_ref, i), head(k_ref, i), 1, 1) * vis_ref[...])
        sc_hi[i], sc_lo[i] = hi, lo
        att[i] = (dot(hi, v, 1, 0) + dot(lo, v, 1, 0)).T
        q_turn[i] = (head(q_ref, i) * first_mask).T
    loads[4].wait()
    loads[5].wait()
    for i in range(heads):
        wgt[i] = (head(gain_ref, i) * head(g_ref, i).astype(F32)).T

    gather_wait(0, piece + 1)
    tags = rcv[0, :, pl.ds(piece, 1)].reshape(nctx, HD)
    firsts = jnp.broadcast_to(tags[:, 0:1], (nctx, HD))
    lasts = jnp.broadcast_to(tags[:, HD - 1 : HD], (nctx, HD))
    outside = jnp.full((1, HD), -1.0, F32)
    before = jnp.concatenate([outside, lasts[: nctx - 1]], axis=0)
    after = jnp.concatenate([firsts[1:], outside], axis=0)
    keep_f[...] = (lasts == before).astype(F32)
    running(0, keep_f, False)
    scatter(1, piece, head_sem.at[1, near])

    keep_b[...] = (firsts == after).astype(F32)
    mine = lax.broadcasted_iota(jnp.int32, (nctx, HD), 0) == me
    tag_in = jnp.max(jnp.where(mine, before, -1.0), axis=0, keepdims=True)
    tag_out = jnp.max(jnp.where(mine, after, -1.0), axis=0, keepdims=True)
    in_mask = (col == tag_in).astype(F32)
    in_bf, out_bf = in_mask.astype(BF16), (col == tag_out).astype(F32).astype(BF16)
    for i in range(heads):
        q_two[i] = twice(head(q_ref, i) * in_bf)
        k_two[i] = twice(head(k_ref, i) * out_bf)
        v_two[i] = twice(head(v_ref, i) * out_bf)

    square = jnp.zeros((HD, rows), F32)
    cross = jnp.zeros((HD, rows), F32)
    for i in near_first:
        head_wait(1, i)
        both = parts(state(1, i).T, 1)
        st[i] = both
        a = att[i] + dot(both, q_two[i], 1, 1)
        att[i] = a
        square += a * a
        cross += a * wgt[i]
    ps_snd[0:1, :] = jnp.sum(square, axis=0, keepdims=True)
    ps_snd[1:2, :] = jnp.sum(cross, axis=0, keepdims=True)
    for d in sorted(range(1, nhead), key=lambda d: -min(d, nhead - d)):
        pltpu.make_async_remote_copy(
            ps_snd, ps_rcv.at[h], ps_sem.at[0], ps_sem.at[1],
            device_id={"head": lax.rem(h + d, nhead)}, device_id_type=MESH,
        ).start()
    ps_rcv[h] = ps_snd[...]
    part = ps_rcv.at[pl.ds(0, nhead - 1)]
    pltpu.make_async_copy(part, part, ps_sem.at[1]).wait()
    sums = jnp.sum(ps_rcv[...], axis=0)
    inv = lax.rsqrt(sums[0:1] / features + EPSILON)
    back = inv * inv * sums[1:2] / features

    rows_of = per // RING
    for i in reversed(near_first):
        both = parts(inv * (wgt[i] - att[i] * back), 0)
        gr[i] = both
        total = dot(q_turn[i], both, 1, 1)
        put_state(2, i, total[:, :HD] + total[:, HD:])
        for dy in sorted(range(RING), key=lambda d: -min(d, RING - d)):
            py = lax.rem(y + turn * dy + RING, RING)
            for r in range(rows_of):
                p = (i * rows_of + lax.rem(z + r, rows_of)) * RING + py
                if i is near_first[0] and dy == 0 and r == 0:
                    keep_own(2, piece, recv_sem.at[2])
                else:
                    send(2, p, piece, recv_sem.at[2])

    def local_grads(i):
        ghi, glo = gr[i, :HD].T, gr[i, HD:].T
        v = head(v_ref, i)
        bhi, blo = split((dot(ghi, v, 1, 1) + dot(glo, v, 1, 1)) * vis_ref[...])
        shi, slo = st[i, :, :HD], st[i, :, HD:]
        gq = dot(ghi, shi, 1, 0) + dot(ghi, slo, 1, 0) + dot(glo, shi, 1, 0)
        gq = (col == tag_in).astype(F32) * gq + dot(bhi, head(k_ref, i), 1, 0) + dot(blo, head(k_ref, i), 1, 0)
        oq_ref[:, pl.ds(i * HD, HD)] = gq.astype(BF16)
        q = head(q_ref, i)
        lk[i] = dot(bhi, q, 0, 0) + dot(blo, q, 0, 0)
        lv[i] = dot(sc_hi[i], ghi, 0, 0) + dot(sc_hi[i], glo, 0, 0) + dot(sc_lo[i], ghi, 0, 0)

    for i in range(heads // 2):
        local_grads(i)

    gather_wait(2, piece)
    running(2, keep_b, True)
    for p in EARLY:
        pl.when(me != p)(functools.partial(send, 3, p, piece, head_sem.at[3, near]))
    for p in peers:
        others = functools.reduce(lambda a, b: a & b, [p != f for f in EARLY])
        pl.when(others)(functools.partial(send, 3, p, piece, head_sem.at[3, near]))
    keep_own(3, piece, head_sem.at[3, near])
    for i in range(heads // 2, heads):
        local_grads(i)
    for i in near_first:
        head_wait(3, i)
        total = state(3, i)
        at = pl.ds(pl.multiple_of(i * HD, HD), HD)
        ok_ref[:, at] = (lk[i] + dot(v_two[i], parts(total, 1), 1, 1)).astype(BF16)
        ov_ref[:, at] = (lv[i] + dot(k_two[i], parts(total, 0), 1, 0)).astype(BF16)

    for phase, size in enumerate((piece + 1, piece, piece, piece)):
        part = snd.at[phase, pl.ds(0, nctx - 1), pl.ds(0, size)]
        pltpu.make_async_copy(part, part, send_sem.at[phase]).wait()
    part = ps_rcv.at[pl.ds(0, nhead - 1)]
    pltpu.make_async_copy(part, part, ps_sem.at[0]).wait()


def write_out(a_ref, b_ref, c_ref, a_hbm, b_hbm, c_hbm, sem):
    copies = [
        pltpu.make_async_copy(src, dst, sem.at[i])
        for i, (src, dst) in enumerate(((a_ref, a_hbm), (b_ref, b_hbm), (c_ref, c_hbm)))
    ]
    for copy in copies:
        copy.start()
    for copy in copies:
        copy.wait()


def solution(mesh):
    nctx, nhead = mesh.shape["ctx"], mesh.shape["head"]

    def on_device(queries, keys, values, out_grad, gain, segment_ids):
        rows, width = queries.shape
        heads = width // HD
        piece = width // nctx
        hbm = pl.BlockSpec(memory_space=pltpu.HBM)
        vmem = pl.BlockSpec(memory_space=pltpu.VMEM)
        wide = pltpu.VMEM((rows, width), BF16)
        total = pltpu.VMEM((heads, rows, HD), F32)
        turned = pltpu.VMEM((heads, HD, rows), F32)
        double = pltpu.VMEM((heads, rows, 2 * HD), BF16)
        arrays = (queries, keys, values, out_grad, gain.reshape(1, width), segment_ids.reshape(1, rows))
        arrays = [pltpu.with_memory_space_constraint(x, pltpu.HBM) for x in arrays]
        grads = pl.pallas_call(
            functools.partial(kernel, nctx, nhead, width * nhead),
            out_shape=[pltpu.VMEM((rows, width), BF16)] * 3,
            in_specs=[hbm] * 6,
            out_specs=[vmem] * 3,
            scratch_shapes=[wide] * 4
            + [
                pltpu.VMEM((1, width), F32),
                pltpu.VMEM((1, rows), jnp.int32),
                pltpu.VMEM((4, nctx, piece + 8, HD), F32),
                pltpu.VMEM((4, nctx, piece + 8, HD), F32),
                pltpu.VMEM((2, rows), F32),
                pltpu.VMEM((nhead, 2, rows), F32),
                pltpu.VMEM((nctx, HD), F32),
                pltpu.VMEM((nctx, HD), F32),
                pltpu.VMEM((rows, rows), F32),
                pltpu.VMEM((heads, rows, rows), BF16),
                pltpu.VMEM((heads, rows, rows), BF16),
                turned,
                turned,
                pltpu.VMEM((heads, 2 * HD, rows), BF16),
                pltpu.VMEM((heads, HD, 2 * HD), BF16),
                total,
                total,
                double,
                pltpu.VMEM((heads, HD, rows), BF16),
                double,
                double,
                pltpu.SemaphoreType.DMA((6,)),
                pltpu.SemaphoreType.DMA((4,)),
                pltpu.SemaphoreType.DMA((4,)),
                pltpu.SemaphoreType.DMA((4, heads)),
                pltpu.SemaphoreType.DMA((2,)),
            ],
            compiler_params=pltpu.CompilerParams(
                collective_id=0, has_side_effects=True, vmem_limit_bytes=40 * 1024 * 1024
            ),
            name="scan_grads",
        )(*arrays)
        return pl.pallas_call(
            write_out,
            out_shape=[jax.ShapeDtypeStruct((rows, width), BF16)] * 3,
            in_specs=[pl.BlockSpec(memory_space=pl.ANY)] * 3,
            out_specs=[hbm] * 3,
            scratch_shapes=[pltpu.SemaphoreType.DMA((3,))],
            name="write_out",
        )(*[pltpu.with_memory_space_constraint(x, pltpu.VMEM) for x in grads])

    return jax.shard_map(
        on_device,
        mesh=mesh,
        in_specs=(
            P("ctx", "head"),
            P("ctx", "head"),
            P("ctx", "head"),
            P("ctx", "head"),
            P("head"),
            P("ctx"),
        ),
        out_specs=(P("ctx", "head"), P("ctx", "head"), P("ctx", "head")),
        check_vma=False,
    )
```
